512 devices in a mesh: rep: 16 (over x, y_lo, core), fsdp: 32 (over z, y_hi).
Axes of the slice: x: 4, y: 8 (y_hi: 4, y_lo: 2; y = y_hi * 2 + y_lo), z: 8, core: 2. Of those that a mesh axis runs over, the one named last changes fastest.
Arguments:
- gradient: bfloat16 [1024, 32768], P('fsdp', 'rep'), may hold values from -6 to 6
- owner_table: int32 [16, 2], replicated, may hold values from 0 to 1, each once within a row
- left_factor: float32 [16, 2048, 1024], P('rep', 'fsdp'), may hold values from -1 to 5
- right_factor: float32 [16, 2048, 1024], P('rep', 'fsdp'), may hold values from -1 to 5
- left_root: bfloat16 [16, 2048, 1024], P('rep', 'fsdp'), may hold values from -1 to 5, as said below
- right_root: bfloat16 [16, 2048, 1024], P('rep', 'fsdp'), may hold values from -1 to 5, as said below
Outputs:
- update: bfloat16 [1024, 32768], P('fsdp')
- left_new: float32 [16, 2048, 1024], P('rep', 'fsdp')
- right_new: float32 [16, 2048, 1024], P('rep', 'fsdp')
The draws below stay inside these ranges and needn't reach their ends.
Inputs may be any that keep to these rules, and one draw needn't show every extreme that they name: `owner_table`: each row is a permutation of the groups. `left_root`: each 1024 x 1024 block of a group is symmetric. `right_root`: each 1024 x 1024 block of a group is symmetric.
All inputs are finite; a program needn't handle non-finite values.
Results may differ from the reference program's by a relative error of at most 0.005.
Values may be sent and summed in bfloat16 or wider, within the bound.
A program may use at most 64 MiB of HBM per device.

```python
import math
import jax
import jax.numpy as jnp
from jax import lax

BS = 1024
NGRP = 2
COLS = 32768
N_REP = 16


def symmetric_blocks(key, diag_low, diag_high, spread):
    noise_key, diag_key = jax.random.split(key)
    noise = jax.random.normal(noise_key, (N_REP, NGRP, BS, BS), jnp.float32)
    mirrored = (noise + jnp.swapaxes(noise, 2, 3)) * (spread / math.sqrt(2.0 * BS))
    diagonal = jnp.exp(jax.random.uniform(diag_key, (N_REP, NGRP, BS, 1), jnp.float32, math.log(diag_low), math.log(diag_high)))
    identity = jnp.eye(BS, dtype=jnp.float32)
    return (mirrored + identity * diagonal).reshape(N_REP, NGRP * BS, BS)


def draw_left_factor(key, part):
    key = jax.random.fold_in(key, 11)
    return symmetric_blocks(key, 0.5, 2.0, 0.3)


def draw_right_factor(key, part):
    key = jax.random.fold_in(key, 12)
    return symmetric_blocks(key, 0.5, 2.0, 0.3)


def draw_left_root(key, part):
    key = jax.random.fold_in(key, 13)
    return symmetric_blocks(key, 1.0, 3.0, 0.4).astype(jnp.bfloat16)


def draw_right_root(key, part):
    key = jax.random.fold_in(key, 14)
    return symmetric_blocks(key, 1.0, 3.0, 0.4).astype(jnp.bfloat16)


def block_levels(stream_key, shape, pieces, least, largest):
    factor_of, own = 1.0, jax.random.fold_in(stream_key, 6)
    for position, parts in pieces:
        heights = jnp.exp(jax.random.uniform(jax.random.fold_in(own, position), (parts,), jnp.float32, least / len(pieces), largest / len(pieces)))
        factor_of = factor_of * jnp.repeat(heights, shape[position] // parts).reshape([-1 if axis == position else 1 for axis in range(len(shape))])
    return factor_of


def bell_draw(rng, dims, scale, limit, cuts=(), kind=jnp.bfloat16):
    array = scale * jax.random.normal(rng, dims, jnp.float32)
    if cuts:
        array = array * block_levels(rng, dims, cuts, -0.22, 0.18)
    return jnp.clip(array, -limit, limit).astype(kind)


def setup_inputs(seed: int = 0) -> dict:
    keys = jax.random.split(jax.random.key(seed), 7)
    return {
        "gradient": bell_draw(keys[0], (BS, COLS), 1.0, 6.0, ((0, 32), (1, 16))),
        "owner_table": jax.vmap(lambda own: jax.random.permutation(own, NGRP))(jax.random.split(keys[1], N_REP)).reshape((N_REP, NGRP)).astype(jnp.int32),
        "left_factor": draw_left_factor(jax.random.fold_in(keys[6], 71), 0),
        "right_factor": draw_right_factor(jax.random.fold_in(keys[6], 71), 0),
        "left_root": draw_left_root(jax.random.fold_in(keys[6], 71), 0),
        "right_root": draw_right_root(jax.random.fold_in(keys[6], 71), 0),
    }


BETA = 0.9
EPSILON = 1e-06

def one_block(items):
    block, left_stat, right_stat, left_inv, right_inv = items
    left_new = BETA * left_stat + (1.0 - BETA) / BS * jnp.dot(block, block.T, preferred_element_type=jnp.float32)
    right_new = BETA * right_stat + (1.0 - BETA) / BS * jnp.dot(block.T, block, preferred_element_type=jnp.float32)
    left_products = jnp.dot(left_inv, block, preferred_element_type=jnp.float32).astype(jnp.bfloat16)
    precond = jnp.dot(left_products, right_inv, preferred_element_type=jnp.float32)
    block_float = block.astype(jnp.float32)
    grad_squares = jnp.sum(block_float * block_float)
    squares = jnp.sum(precond * precond)
    scaled = (precond * (jnp.sqrt(grad_squares) / jnp.sqrt(squares + EPSILON))).astype(jnp.bfloat16)
    return (scaled, left_new, right_new)

def reference(gradient, owner_table, left_factor, right_factor, left_root, right_root):
    count = N_REP * NGRP
    blocks = gradient.reshape(BS, N_REP, NGRP, BS).transpose(1, 2, 0, 3)
    positions = jnp.arange(NGRP, dtype=jnp.int32)
    match = owner_table[:, None, :] == positions[None, :, None]
    inverse = lax.optimization_barrier(jnp.sum(jnp.where(match, positions[None, None, :], 0), axis=2)).astype(jnp.int32)
    by_group = jax.vmap(lambda part, order: jnp.take(part, order, axis=0))(blocks, inverse)
    scaled, left_new, right_new = lax.map(one_block, (by_group.reshape(count, BS, BS), left_factor.reshape(count, BS, BS), right_factor.reshape(count, BS, BS), left_root.reshape(count, BS, BS), right_root.reshape(count, BS, BS)))
    grouped = scaled.reshape(N_REP, NGRP, BS, BS)
    placed = jax.vmap(lambda part, order: jnp.take(part, order, axis=0))(grouped, owner_table)
    update = placed.transpose(2, 0, 1, 3).reshape(BS, N_REP * NGRP * BS)
    return (update, left_new.reshape(N_REP, NGRP * BS, BS), right_new.reshape(N_REP, NGRP * BS, BS))
```

```python
import jax
import jax.numpy as jnp
from jax import lax
from jax.experimental import pallas as pl
from jax.experimental.pallas import tpu as pltpu
from jax.sharding import PartitionSpec as P

BETA = 0.9
EPSILON = 1e-06
MESH = pl.DeviceIdType.MESH
F32 = jnp.float32
BF16 = jnp.bfloat16
NT = (((1,), (1,)), ((), ()))


def kernel(
    grad_in, table, lf_in, rf_in, lr_in, rr_in,
    upd_out, left_out, right_out,
    raw, other, gbuf, abuf, bbuf, lbuf, pbuf, home, ubuf, lf, rf, wide, scy, sct, sch,
    lsem, ssem, rsem, hsem, zsem, hsend, zsend,
):
    r = lax.axis_index("rep")
    f = lax.axis_index("fsdp")
    z, y = f // 4, f % 4
    g, p = z // 4, z % 4
    x, yl, c = r // 4, (r // 2) % 2, r % 2
    yn, yp, yo = (y + 1) % 4, (y + 3) % 4, (y + 2) % 4
    zm = 7 - z

    def fdev(zz, yy):
        return {"fsdp": zz * 4 + yy}

    up, down, north, south, mirror = fdev((z + 1) % 8, y), fdev((z + 7) % 8, y), fdev(z, yn), fdev(z, yp), fdev(zm, y)
    r_sib, r_ylo = r + 1 - 2 * c, r + 2 - 4 * yl
    r_xp, r_xm = ((x + 1) % 4) * 4 + r % 4, ((x + 3) % 4) * 4 + r % 4
    sib, ylo, xp, xm = {"rep": r_sib}, {"rep": r_ylo}, {"rep": r_xp}, {"rep": r_xm}

    def load(src, dst, k):
        copy = pltpu.make_async_copy(src, dst, lsem.at[k])
        copy.start()
        return copy

    ld_g = load(grad_in, raw, 0)
    ld_a = load(lr_in.at[0], abuf.at[p], 1)
    ld_b = load(rr_in.at[0], bbuf.at[y], 2)
    ld_l = load(lf_in.at[0], lf, 3)
    ld_r = load(rf_in.at[0], rf, 4)

    barrier = pltpu.get_barrier_semaphore()
    near = (up, down, north, south, mirror, sib, ylo, xp, xm)
    for dev in near:
        pl.semaphore_signal(barrier, inc=1, device_id=dev, device_id_type=MESH)

    pending = []
    counter = [0, 0]

    def new_recv():
        counter[1] += 1
        return rsem.at[counter[1] - 1]

    def send(src, dst, dev, arrival, pred=None):
        copy = pltpu.make_async_remote_copy(
            src_ref=src, dst_ref=dst, send_sem=ssem.at[counter[0]], recv_sem=arrival,
            device_id=dev, device_id_type=MESH,
        )
        counter[0] += 1
        if pred is None:
            copy.start()
        else:
            pl.when(pred)(copy.start)
        pending.append((copy, pred))

    def arrive(dst, arrival, pred=None):
        copy = pltpu.make_async_remote_copy(
            src_ref=dst, dst_ref=dst, send_sem=ssem.at[0], recv_sem=arrival,
            device_id=north, device_id_type=MESH,
        )
        if pred is None:
            copy.wait_recv()
        else:
            pl.when(pred)(copy.wait_recv)

    class Line:
        def __init__(self, slot):
            self.slot = slot
            self.plus = [None] + [new_recv() for _ in range(3)]
            self.minus = [None] + [new_recv() for _ in range(3)]

        def hop(self, d):
            if d >= 2:
                arrive(self.slot(jnp.maximum(z - d + 1, 0)), self.plus[d - 1], p >= d - 1)
            if d <= 3:
                src = self.slot(jnp.maximum(z - d + 1, 0))
                send(src, src, up, self.plus[d], (p >= d - 1) & (p <= 2))
            if d >= 2:
                arrive(self.slot(jnp.minimum(z + d - 1, 7)), self.minus[d - 1], p <= 4 - d)
            if d <= 3:
                src = self.slot(jnp.minimum(z + d - 1, 7))
                send(src, src, down, self.minus[d], (p <= 4 - d) & (p >= 1))

    class Ring:
        def __init__(self, slot, first, second):
            self.slot, self.first, self.second = slot, first, second
            self.sems = [new_recv() for _ in range(4)]

        def start(self):
            for dev, sem in ((north, self.sems[0]), (south, self.sems[1])):
                send(self.slot(y), self.slot(y), dev, sem)

        def forward(self):
            arrive(self.slot(yp), self.sems[0])
            if self.first is not None:
                send(self.first(yp), self.first(yp), north, self.sems[2])
            arrive(self.slot(yn), self.sems[1])
            if self.second is not None:
                send(self.second(yn), self.second(yn), south, self.sems[3])

        def finish(self):
            if self.first is not None:
                arrive(self.first(yo), self.sems[2])
            if self.second is not None:
                arrive(self.second(yo), self.sems[3])

    ld_g.wait()
    swap = table[r, 0] != 0
    first_is_mine = jnp.where(swap, g == 1, g == 0)
    lo, hi = raw[:, 0:1024], raw[:, 1024:2048]
    mine = jnp.where(first_is_mine, lo, hi)
    theirs = jnp.where(first_is_mine, hi, lo)
    for h in range(2):
        gbuf[h, z, y] = mine[:, 512 * h:512 * h + 512]
        other[h] = theirs[:, 512 * h:512 * h + 512]

    pl.semaphore_wait(barrier, len(near))

    esem = [new_recv() for _ in range(2)]
    for h in range(2):
        send(other.at[h], gbuf.at[h, z, y], mirror, esem[h])

    def slot0(zz):
        return lambda yy: gbuf.at[0, zz, yy]

    ring_a = Ring(slot0(z), slot0(z), None)
    ring_b = Ring(slot0(zm), None, slot0(zm))
    line_a = Line(lambda zz: gbuf.at[1, zz, y])
    line_b = Line(lambda zz: gbuf.at[1, 7 - zz, y])
    slab_a = Line(lambda zz: gbuf.at[0, zz])
    slab_b = Line(lambda zz: gbuf.at[0, 7 - zz])
    ring_s = Ring(
        lambda yy: gbuf.at[1, :, yy],
        lambda yy: gbuf.at[1, pl.ds(0, 4), yy],
        lambda yy: gbuf.at[1, pl.ds(4, 4), yy],
    )
    line_r = Line(lambda zz: abuf.at[zz % 4])
    ring_r = Ring(
        lambda yy: bbuf.at[yy],
        lambda yy: bbuf.at[yy, pl.ds(0, 32)],
        lambda yy: bbuf.at[yy, pl.ds(32, 32)],
    )

    ring_a.start()
    line_a.hop(1)
    arrive(gbuf.at[0, zm, y], esem[0])
    ring_b.start()
    arrive(gbuf.at[1, zm, y], esem[1])
    line_b.hop(1)
    ring_a.forward()
    line_a.hop(2)
    ring_b.forward()
    line_b.hop(2)
    ring_a.finish()
    slab_a.hop(1)
    ring_b.finish()
    slab_b.hop(1)
    line_a.hop(3)
    line_b.hop(3)
    line_a.hop(4)
    line_b.hop(4)
    ring_s.start()
    ld_a.wait()
    line_r.hop(1)
    ld_b.wait()
    ring_r.start()
    slab_a.hop(2)
    slab_b.hop(2)
    ring_s.forward()
    slab_a.hop(3)
    slab_b.hop(3)
    line_r.hop(2)
    ring_r.forward()
    line_r.hop(3)
    line_r.hop(4)
    slab_a.hop(4)
    slab_b.hop(4)

    def left_half(h):
        def step(t, _):
            cols = pl.ds(pl.multiple_of(t * 256, 256), 256)
            g_cols = gbuf[h, :, :, :, cols].reshape(1024, 256)
            prod = jnp.dot(abuf[...].reshape(256, 1024), g_cols, preferred_element_type=F32)
            lbuf[:, pl.ds(pl.multiple_of(512 * h + t * 256, 256), 256)] = prod.astype(BF16)
            return 0
        lax.fori_loop(0, 2, step, 0)

    left_half(0)
    ring_s.finish()
    left_half(1)
    ring_r.finish()
    prod = lax.dot_general(lbuf[...], bbuf[...].reshape(256, 1024), NT, preferred_element_type=F32)
    pbuf[...] = prod.astype(BF16).reshape(4, 2, 32, 256)

    homes = [(2 * q + y // 2, 2 * (y % 2) + j, q, j) for q in range(4) for j in range(2)]
    me = 4 * g + p
    mycols = pl.ds(pl.multiple_of(256 * p, 256), 256)

    def to_homes(pick, place, arrivals, sends):
        for k, (hz, hy, q, j) in enumerate(homes):
            itself = (hz == z) & (hy == y)
            away = pltpu.make_async_remote_copy(
                src_ref=pick(q, j), dst_ref=place, send_sem=sends.at[k], recv_sem=arrivals.at[me],
                device_id=fdev(hz, hy), device_id_type=MESH,
            )
            here = pltpu.make_async_copy(pick(q, j), place, arrivals.at[me])
            pl.when(itself)(here.start)
            pl.when(jnp.logical_not(itself))(away.start)
            pending.append((away, jnp.logical_not(itself)))

    to_homes(lambda q, j: pbuf.at[q, j], home.at[g, :, mycols], hsem, hsend)

    squares = jnp.sum(jnp.sum(prod * prod, axis=0, keepdims=True), axis=1, keepdims=True)
    scy[y] = jnp.broadcast_to(squares, (8, 128))
    ysem = [new_recv() for _ in range(3)]
    for d in range(1, 4):
        send(scy.at[y], scy.at[y], fdev(z, (y + d) % 4), ysem[d - 1])

    def add_squares(t, total):
        part = gbuf[t // 8, t % 8].reshape(128, 512).astype(F32)
        return total + jnp.sum(part * part, axis=0, keepdims=True)

    grad_squares = lax.fori_loop(0, 16, add_squares, jnp.zeros((1, 512), F32))
    sct[1] = jnp.broadcast_to(jnp.sum(grad_squares, axis=1, keepdims=True), (8, 128))
    for d in range(1, 4):
        arrive(scy.at[(y + 4 - d) % 4], ysem[d - 1])
    sct[0] = scy[0] + scy[1] + scy[2] + scy[3]
    to_homes(lambda q, j: sct, sch.at[me], zsem, zsend)

    ld_l.wait()
    own = [gbuf[h, 2 * p + y // 2, pl.ds(2 * (y % 2), 2)].reshape(64, 512) for h in range(2)]
    for t in range(4):
        stat = jnp.zeros((64, 256), F32)
        for h in range(2):
            rows = gbuf[h, pl.ds(2 * t, 2)].reshape(256, 512)
            stat = stat + lax.dot_general(own[h], rows, NT, preferred_element_type=F32)
        cols = slice(256 * t, 256 * t + 256)
        lf[:, cols] = BETA * lf[:, cols] + (1.0 - BETA) / 1024 * stat
    st_l = pltpu.make_async_copy(lf, left_out.at[0], lsem.at[3])
    st_l.start()

    for k in range(8):
        arrive(home.at[k // 4, :, pl.ds(256 * (k % 4), 256)], hsem.at[k])
    for k in range(8):
        arrive(sch.at[k], zsem.at[k])
    done = []
    for q in range(2):
        total = sch[4 * q, 0] + sch[4 * q + 1, 0] + sch[4 * q + 2, 0] + sch[4 * q + 3, 0]
        ratio = jnp.sqrt(sch[4 * q, 1]) / jnp.sqrt(total + EPSILON)
        done.append((home[q].astype(F32) * ratio[0:1, 0:1]).astype(BF16))

    def slot(rr):
        return ubuf.at[:, pl.ds(pl.multiple_of(rr * 2048, 2048), 2048)]

    def part(rr, k):
        return ubuf.at[pl.ds(16 * k, 16), pl.ds(pl.multiple_of(rr * 2048, 2048), 2048)]

    ubuf[:, pl.ds(pl.multiple_of(r * 2048, 2048), 1024)] = jnp.where(swap, done[1], done[0])
    ubuf[:, pl.ds(pl.multiple_of(r * 2048 + 1024, 1024), 1024)] = jnp.where(swap, done[0], done[1])

    sib_waits = []

    def share(ref_of, rr):
        sem = new_recv()
        send(ref_of(rr), ref_of(rr), sib, sem)
        sib_waits.append((ref_of(rr + 1 - 2 * c), sem))

    y_sem = new_recv()
    xps, xms, xpf, xmf = ([new_recv() for _ in range(2)] for _ in range(4))
    send(slot(r), slot(r), ylo, y_sem)
    send(slot(r), slot(r), xp, xps[0])
    send(slot(r), slot(r), xm, xms[0])
    share(slot, r)

    def rep_of(q, dx):
        return ((x + dx + 4) % 4) * 4 + (yl + q - 2 * yl * q) * 2 + c

    arrive(slot(r_ylo), y_sem)
    send(slot(r_ylo), slot(r_ylo), xp, xps[1])
    send(slot(r_ylo), slot(r_ylo), xm, xms[1])
    share(slot, r_ylo)
    for q in range(2):
        before, after = rep_of(q, -1), rep_of(q, 1)
        arrive(slot(before), xps[q])
        send(part(before, 0), part(before, 0), xp, xpf[q])
        share(slot, before)
        arrive(slot(after), xms[q])
        send(part(after, 1), part(after, 1), xm, xmf[q])
        share(slot, after)

    ld_r.wait()
    lanes = pl.ds(pl.multiple_of(128 * (2 * (p % 2) + y // 2), 128), 128)
    turned = gbuf[p // 2, :, :, :, lanes].reshape(1024, 128).T
    for t in range(4):
        g_cols = gbuf[t // 2, :, :, :, 256 * (t % 2):256 * (t % 2) + 256].reshape(1024, 256)
        wide[:, 256 * t:256 * t + 256] = jnp.dot(turned, g_cols, preferred_element_type=F32)
    rf[...] = BETA * rf[...] + (1.0 - BETA) / 1024 * wide[pl.ds(pl.multiple_of(64 * (y % 2), 64), 64), :]
    st_r = pltpu.make_async_copy(rf, right_out.at[0], lsem.at[4])
    st_r.start()

    for q in range(2):
        across = rep_of(q, 2)
        arrive(part(across, 0), xpf[q])
        share(lambda rr: part(rr, 0), across)
        arrive(part(across, 1), xmf[q])
        share(lambda rr: part(rr, 1), across)
    for ref, sem in sib_waits:
        arrive(ref, sem)
    st_u = pltpu.make_async_copy(ubuf, upd_out, lsem.at[0])
    st_u.start()
    for copy, pred in pending:
        if pred is None:
            copy.wait_send()
        else:
            pl.when(pred)(copy.wait_send)
    st_l.wait()
    st_r.wait()
    st_u.wait()


def body(gradient, owner_table, left_factor, right_factor, left_root, right_root):
    vmem = pltpu.VMEM
    anywhere = pl.BlockSpec(memory_space=pl.ANY)
    return pl.pallas_call(
        kernel,
        out_shape=(
            jax.ShapeDtypeStruct((32, 32768), BF16),
            jax.ShapeDtypeStruct((1, 64, 1024), F32),
            jax.ShapeDtypeStruct((1, 64, 1024), F32),
        ),
        in_specs=[anywhere, pl.BlockSpec(memory_space=pltpu.SMEM)] + [anywhere] * 4,
        out_specs=(anywhere,) * 3,
        scratch_shapes=[
            vmem((32, 2048), BF16),
            vmem((2, 32, 512), BF16),
            vmem((2, 8, 4, 32, 512), BF16),
            vmem((4, 64, 1024), BF16),
            vmem((4, 64, 1024), BF16),
            vmem((256, 1024), BF16),
            vmem((4, 2, 32, 256), BF16),
            vmem((2, 32, 1024), BF16),
            vmem((32, 32768), BF16),
            vmem((64, 1024), F32),
            vmem((64, 1024), F32),
            vmem((128, 1024), F32),
            vmem((4, 8, 128), F32),
            vmem((2, 8, 128), F32),
            vmem((8, 2, 8, 128), F32),
            pltpu.SemaphoreType.DMA((5,)),
            pltpu.SemaphoreType.DMA((80,)),
            pltpu.SemaphoreType.DMA((80,)),
            pltpu.SemaphoreType.DMA((8,)),
            pltpu.SemaphoreType.DMA((8,)),
            pltpu.SemaphoreType.DMA((8,)),
            pltpu.SemaphoreType.DMA((8,)),
        ],
        compiler_params=pltpu.CompilerParams(
            collective_id=0, has_side_effects=True, vmem_limit_bytes=40 * 1024 * 1024
        ),
    )(gradient, owner_table, left_factor, right_factor, left_root, right_root)


def solution(mesh):
    placed = (
        P("fsdp", "rep"),
        P(),
        P("rep", "fsdp", None),
        P("rep", "fsdp", None),
        P("rep", "fsdp", None),
        P("rep", "fsdp", None),
    )
    return jax.shard_map(
        body,
        mesh=mesh,
        in_specs=placed,
        out_specs=(P("fsdp", None), P("rep", "fsdp", None), P("rep", "fsdp", None)),
        check_vma=False,
    )
```

```python
import jax
import jax.numpy as jnp
from jax import lax
from jax.experimental import pallas as pl
from jax.experimental.pallas import tpu as pltpu
from jax.sharding import PartitionSpec as P

BETA = 0.9
EPSILON = 1e-06
MESH = pl.DeviceIdType.MESH
F32 = jnp.float32
BF16 = jnp.bfloat16
NT = (((1,), (1,)), ((), ()))


def kernel(
    grad_in, table_in, lf_in, rf_in, lr_in, rr_in,
    upd, left_out, right_out,
    table, raw, strips, gbuf, abuf, bbuf, lbuf, pbuf, home, own, lf, rf, wide, sums,
    lsem, ssem, rsem, hsem, zsem, hsend,
):
    r = lax.axis_index("rep")
    f = lax.axis_index("fsdp")
    z, y = f // 4, f % 4
    g, p = z // 4, z % 4
    x, yl, c = r // 4, (r // 2) % 2, r % 2
    yn, yp, yo = (y + 1) % 4, (y + 3) % 4, (y + 2) % 4

    def fdev(zz, yy):
        return {"fsdp": zz * 4 + yy}

    up, down, north, south = fdev((z + 1) % 8, y), fdev((z + 7) % 8, y), fdev(z, yn), fdev(z, yp)
    r_sib, r_ylo = r + 1 - 2 * c, r + 2 - 4 * yl
    sib, ylo = {"rep": r_sib}, {"rep": r_ylo}
    xp, xm, xo = ({"rep": ((x + d) % 4) * 4 + r % 4} for d in (1, 3, 2))

    barrier = pltpu.get_barrier_semaphore()
    near = [fdev((z + d) % 8, y) for d in (1, 7, 2, 6, 3, 5, 4)] + [north, south, sib, ylo, xp, xm, xo]
    for dev in near:
        pl.semaphore_signal(barrier, inc=1, device_id=dev, device_id_type=MESH)

    def load(src, dst, k):
        copy = pltpu.make_async_copy(src, dst, lsem.at[k])
        copy.start()
        return copy

    ld_g = load(grad_in, raw, 0)
    ld_t = load(table_in, table, 5)
    ld_a = load(lr_in.at[0], abuf.at[p], 1)
    ld_b = load(rr_in.at[0], bbuf.at[y], 2)
    ld_l = load(lf_in.at[0], lf, 3)
    ld_r = load(rf_in.at[0], rf, 4)

    pending = []
    counter = [0, 0]

    def new_recv():
        counter[1] += 1
        return rsem.at[counter[1] - 1]

    def send(src, dst, dev, arrival, pred=None):
        copy = pltpu.make_async_remote_copy(
            src_ref=src, dst_ref=dst, send_sem=ssem.at[counter[0]], recv_sem=arrival,
            device_id=dev, device_id_type=MESH,
        )
        counter[0] += 1
        if pred is None:
            copy.start()
        else:
            pl.when(pred)(copy.start)
        pending.append((copy, pred))

    def arrive(dst, arrival, pred=None):
        copy = pltpu.make_async_remote_copy(
            src_ref=dst, dst_ref=dst, send_sem=ssem.at[0], recv_sem=arrival,
            device_id=north, device_id_type=MESH,
        )
        if pred is None:
            copy.wait_recv()
        else:
            pl.when(pred)(copy.wait_recv)

    class Line:
        def __init__(self, slot):
            self.slot = slot
            self.plus = [None] + [new_recv() for _ in range(3)]
            self.minus = [None] + [new_recv() for _ in range(3)]

        def hop(self, d):
            if d >= 2:
                arrive(self.slot(jnp.maximum(z - d + 1, 0)), self.plus[d - 1], p >= d - 1)
            if d <= 3:
                src = self.slot(jnp.maximum(z - d + 1, 0))
                send(src, src, up, self.plus[d], (p >= d - 1) & (p <= 2))
            if d >= 2:
                arrive(self.slot(jnp.minimum(z + d - 1, 7)), self.minus[d - 1], p <= 4 - d)
            if d <= 3:
                src = self.slot(jnp.minimum(z + d - 1, 7))
                send(src, src, down, self.minus[d], (p <= 4 - d) & (p >= 1))

    class Ring:
        def __init__(self, slot, first, second):
            self.slot, self.first, self.second = slot, first, second
            self.sems = [new_recv() for _ in range(4)]

        def start(self):
            for dev, sem in ((north, self.sems[0]), (south, self.sems[1])):
                send(self.slot(y), self.slot(y), dev, sem)

        def forward(self):
            arrive(self.slot(yp), self.sems[0])
            send(self.first(yp), self.first(yp), north, self.sems[2])
            arrive(self.slot(yn), self.sems[1])
            send(self.second(yn), self.second(yn), south, self.sems[3])

        def finish(self):
            arrive(self.first(yo), self.sems[2])
            arrive(self.second(yo), self.sems[3])

    ld_g.wait()
    ld_t.wait()
    swap = table[0, r] != 0
    lo, hi = raw[:, 0:1024], raw[:, 1024:2048]
    for q in range(2):
        block = jnp.where(swap, hi, lo) if q == 0 else jnp.where(swap, lo, hi)
        for s in range(4):
            strips[4 * q + s] = block[:, 256 * s:256 * s + 256]
    gbuf[p, z, y] = strips[z]

    pl.semaphore_wait(barrier, len(near))

    asem = [new_recv() for _ in range(8)]
    for d in (4, 3, 5, 2, 6, 1, 7):
        zz = (z + d) % 8
        send(strips.at[zz], gbuf.at[zz % 4, z, y], fdev(zz, y), asem[d])

    def ring_of(s):
        return Ring(
            lambda yy: gbuf.at[s, :, yy],
            lambda yy: gbuf.at[s, pl.ds(0, 4), yy],
            lambda yy: gbuf.at[s, pl.ds(4, 4), yy],
        )

    ring_p = ring_of(p)
    others = [(p + d) % 4 for d in range(1, 4)]
    rings = [ring_of(s) for s in others]
    line_r = Line(lambda zz: abuf.at[zz % 4])
    line_g = Line(lambda zz: gbuf.at[zz % 4, :, y])
    ring_r = Ring(
        lambda yy: bbuf.at[yy],
        lambda yy: bbuf.at[yy, pl.ds(0, 32)],
        lambda yy: bbuf.at[yy, pl.ds(32, 32)],
    )

    ld_a.wait()
    line_r.hop(1)
    ld_b.wait()
    ring_r.start()
    for d in (1, 7, 2, 6, 3, 5, 4):
        arrive(gbuf.at[p, (z + 8 - d) % 8, y], asem[d])
    ring_p.start()
    line_g.hop(1)
    line_r.hop(2)
    ring_r.forward()
    line_r.hop(3)
    line_g.hop(2)
    ring_p.forward()
    line_r.hop(4)
    line_g.hop(3)
    ring_p.finish()

    lbuf[p] = jnp.dot(
        abuf[...].reshape(256, 1024), gbuf[p].reshape(1024, 256), preferred_element_type=F32
    ).astype(BF16)
    psem = [new_recv() for _ in range(4)]
    for d in (1, 3, 2):
        send(lbuf.at[p], lbuf.at[p], fdev(4 * g + (p + d) % 4, y), psem[d])
    line_g.hop(4)
    for ring in rings:
        ring.start()

    def add_squares(t, total):
        part = gbuf[p, t].reshape(128, 256).astype(F32)
        return total + jnp.sum(part * part, axis=0, keepdims=True)

    grad_squares = lax.fori_loop(0, 8, add_squares, jnp.zeros((1, 256), F32))
    grad_squares = 0.25 * jnp.sum(grad_squares, axis=1, keepdims=True)

    scale = (1.0 - BETA) / 1024
    my_z, my_y = 2 * p + y // 2, 2 * (y % 2)
    lanes = pl.ds(pl.multiple_of(128 * (y // 2), 128), 128)

    def statistics(s):
        mine = gbuf[s, my_z, pl.ds(my_y, 2)].reshape(64, 256)
        for t in range(4):
            rows = gbuf[s, pl.ds(2 * t, 2)].reshape(256, 256)
            lf[:, 256 * t:256 * t + 256] += scale * lax.dot_general(mine, rows, NT, preferred_element_type=F32)
        turned = gbuf[p, :, :, :, lanes].reshape(1024, 128).T
        wide[...] = jnp.dot(turned, gbuf[s].reshape(1024, 256), preferred_element_type=F32)
        cols = pl.ds(pl.multiple_of(256 * s, 256), 256)
        rf[:, cols] = BETA * rf[:, cols] + scale * wide[pl.ds(pl.multiple_of(64 * (y % 2), 64), 64), :]

    ld_l.wait()
    ld_r.wait()
    lf[...] = BETA * lf[...]
    statistics(p)
    ring_r.finish()

    def tile_part(s):
        cols = pl.ds(pl.multiple_of(256 * s, 256), 256)
        return lax.dot_general(lbuf[s], bbuf[:, :, cols].reshape(256, 256), NT, preferred_element_type=F32)

    prod = tile_part(p)
    for d in (1, 3, 2):
        s = (p + 4 - d) % 4
        arrive(lbuf.at[s], psem[d])
        prod = prod + tile_part(s)
    pbuf[...] = prod.astype(BF16).reshape(4, 2, 32, 256)

    mycols = pl.ds(pl.multiple_of(256 * p, 256), 256)
    for q in range(4):
        for j in range(2):
            k, hz, hy = 2 * q + j, 2 * q + y // 2, 2 * (y % 2) + j
            itself = (hz == z) & (hy == y)
            src, place, arrival = pbuf.at[q, j], home.at[g, :, mycols], hsem.at[4 * g + p]
            away = pltpu.make_async_remote_copy(
                src_ref=src, dst_ref=place, send_sem=hsend.at[k], recv_sem=arrival,
                device_id=fdev(hz, hy), device_id_type=MESH,
            )
            here = pltpu.make_async_copy(src, place, arrival)
            pl.when(itself)(here.start)
            pl.when(jnp.logical_not(itself))(away.start)
            pending.append((away, jnp.logical_not(itself)))
    squares = jnp.sum(jnp.sum(prod * prod, axis=0, keepdims=True), axis=1, keepdims=True)
    row = lax.broadcasted_iota(jnp.int32, (8, 128), 0)
    sums[f] = jnp.where(row < 4, squares, grad_squares)

    def tell(d, _):
        pltpu.make_async_remote_copy(
            src_ref=sums.at[f], dst_ref=sums.at[f], send_sem=zsem.at[0], recv_sem=zsem.at[1],
            device_id={"fsdp": (f + d) % 32}, device_id_type=MESH,
        ).start()
        return 0

    lax.fori_loop(1, 32, tell, 0)
    rings[0].forward()

    for k in range(8):
        arrive(home.at[k // 4, :, pl.ds(256 * (k % 4), 256)], hsem.at[k])
    everyone = pltpu.make_async_remote_copy(
        src_ref=sums.at[pl.ds(0, 31)], dst_ref=sums.at[pl.ds(0, 31)], send_sem=zsem.at[0], recv_sem=zsem.at[1],
        device_id=north, device_id_type=MESH,
    )
    everyone.wait_recv()
    done = []
    for q in range(2):
        total = jnp.sum(sums[16 * q:16 * q + 16], axis=0)
        ratio = jnp.sqrt(total[4:5, 0:1]) / jnp.sqrt(total[0:1, 0:1] + EPSILON)
        done.append((home[q].astype(F32) * ratio).astype(BF16))
    own[:, 0:1024] = jnp.where(swap, done[1], done[0])
    own[:, 1024:2048] = jnp.where(swap, done[0], done[1])

    def slot(rr):
        return upd.at[:, pl.ds(pl.multiple_of(rr * 2048, 2048), 2048)]

    sib_waits = []

    def share(rr, src=None):
        sem = new_recv()
        send(slot(rr) if src is None else src, slot(rr), sib, sem)
        sib_waits.append((slot(rr + 1 - 2 * c), sem))

    def rep_of(q, dx):
        return ((x + dx + 4) % 4) * 4 + (yl + q - 2 * yl * q) * 2 + c

    y_sem = new_recv()
    xsem = [[new_recv() for _ in range(4)] for _ in range(2)]
    send(own, slot(r), ylo, y_sem)
    for d in (1, 3, 2):
        send(own, slot(r), {"rep": rep_of(0, d)}, xsem[0][d])
    share(r, own)
    keep = pltpu.make_async_copy(own, slot(r), lsem.at[0])
    keep.start()
    rings[1].forward()
    arrive(slot(r_ylo), y_sem)
    for d in (1, 3, 2):
        send(slot(r_ylo), slot(r_ylo), {"rep": rep_of(0, d)}, xsem[1][d])
    share(r_ylo)
    rings[2].forward()
    for q in range(2):
        for d in (1, 3, 2):
            arrive(slot(rep_of(q, -d)), xsem[q][d])
            share(rep_of(q, -d))
    for ring, s in zip(rings, others):
        ring.finish()
        statistics(s)
    st_l = pltpu.make_async_copy(lf, left_out.at[0], lsem.at[3])
    st_l.start()
    st_r = pltpu.make_async_copy(rf, right_out.at[0], lsem.at[4])
    st_r.start()
    for ref, sem in sib_waits:
        arrive(ref, sem)
    for copy, pred in pending:
        if pred is None:
            copy.wait_send()
        else:
            pl.when(pred)(copy.wait_send)
    everyone.wait_send()
    keep.wait()
    st_l.wait()
    st_r.wait()


def pinned(array):
    return pltpu.with_memory_space_constraint(array, pltpu.HBM)


def body(gradient, owner_table, left_factor, right_factor, left_root, right_root):
    vmem = pltpu.VMEM
    anywhere = pl.BlockSpec(memory_space=pl.ANY)
    hbm = pl.BlockSpec(memory_space=pltpu.HBM)
    return pl.pallas_call(
        kernel,
        out_shape=(
            vmem((32, 32768), BF16),
            vmem((1, 64, 1024), F32),
            vmem((1, 64, 1024), F32),
        ),
        in_specs=[hbm] * 6,
        out_specs=(anywhere,) * 3,
        scratch_shapes=[
            pltpu.SMEM((2, 16), jnp.int32),
            vmem((32, 2048), BF16),
            vmem((8, 32, 256), BF16),
            vmem((4, 8, 4, 32, 256), BF16),
            vmem((4, 64, 1024), BF16),
            vmem((4, 64, 1024), BF16),
            vmem((4, 256, 256), BF16),
            vmem((4, 2, 32, 256), BF16),
            vmem((2, 32, 1024), BF16),
            vmem((32, 2048), BF16),
            vmem((64, 1024), F32),
            vmem((64, 1024), F32),
            vmem((128, 256), F32),
            vmem((32, 8, 128), F32),
            pltpu.SemaphoreType.DMA((6,)),
            pltpu.SemaphoreType.DMA((80,)),
            pltpu.SemaphoreType.DMA((80,)),
            pltpu.SemaphoreType.DMA((8,)),
            pltpu.SemaphoreType.DMA((2,)),
            pltpu.SemaphoreType.DMA((8,)),
        ],
        compiler_params=pltpu.CompilerParams(
            collective_id=0, has_side_effects=True, vmem_limit_bytes=40 * 1024 * 1024
        ),
    )(
        pinned(gradient), pinned(owner_table.T), pinned(left_factor), pinned(right_factor),
        pinned(left_root), pinned(right_root),
    )


def solution(mesh):
    placed = (
        P("fsdp", "rep"),
        P(),
        P("rep", "fsdp", None),
        P("rep", "fsdp", None),
        P("rep", "fsdp", None),
        P("rep", "fsdp", None),
    )
    return jax.shard_map(
        body,
        mesh=mesh,
        in_specs=placed,
        out_specs=(P("fsdp", None), P("rep", "fsdp", None), P("rep", "fsdp", None)),
        check_vma=False,
    )
```

```python
import jax
import jax.numpy as jnp
from jax import lax
from jax.experimental import pallas as pl
from jax.experimental.pallas import tpu as pltpu
from jax.sharding import PartitionSpec as P

BETA = 0.9
EPSILON = 1e-06
MESH = pl.DeviceIdType.MESH
F32 = jnp.float32
BF16 = jnp.bfloat16
NT = (((1,), (1,)), ((), ()))


def kernel(
    grad_in, table_in, lf_in, rf_in, lr_in, rr_in,
    upd, lf_out, rf_out,
    table, raw, strips, gbuf, abuf, bbuf, lbuf, pbuf, land, wide, sum_y, sum_z, ratio,
    lsem, ssem, rsem, hsem, tsem, hsend,
):
    r = lax.axis_index("rep")
    f = lax.axis_index("fsdp")
    z, y = f // 4, f % 4
    g, p = z // 4, z % 4
    x, yl, c = r // 4, (r // 2) % 2, r % 2
    yn, yp, yo = (y + 1) % 4, (y + 3) % 4, (y + 2) % 4

    def fdev(zz, yy):
        return {"fsdp": zz * 4 + yy}

    up, down, north, south = fdev((z + 1) % 8, y), fdev((z + 7) % 8, y), fdev(z, yn), fdev(z, yp)
    r_sib, r_ylo = r + 1 - 2 * c, r + 2 - 4 * yl
    sib, ylo = {"rep": r_sib}, {"rep": r_ylo}

    barrier = pltpu.get_barrier_semaphore()
    near = [fdev((z + d) % 8, y) for d in (1, 7, 2, 6, 3, 5, 4)] + [north, south]
    near += [{"rep": (r + d) % 16} for d in range(1, 16)]
    for dev in near:
        pl.semaphore_signal(barrier, inc=1, device_id=dev, device_id_type=MESH)

    def load(src, dst, k):
        copy = pltpu.make_async_copy(src, dst, lsem.at[k])
        copy.start()
        return copy

    ld_g = load(grad_in, raw, 0)
    ld_t = load(table_in, table, 5)
    ld_a = load(lr_in.at[0], abuf.at[p], 1)
    ld_b = load(rr_in.at[0], bbuf.at[y], 2)
    lf, rf = lf_out.at[0], rf_out.at[0]
    ld_l = load(lf_in.at[0], lf, 3)
    ld_r = load(rf_in.at[0], rf, 4)

    pending = []
    counter = [0, 0]

    def new_recv():
        counter[1] += 1
        return rsem.at[counter[1] - 1]

    def send(src, dst, dev, arrival, pred=None):
        copy = pltpu.make_async_remote_copy(
            src_ref=src, dst_ref=dst, send_sem=ssem.at[counter[0]], recv_sem=arrival,
            device_id=dev, device_id_type=MESH,
        )
        counter[0] += 1
        if pred is None:
            copy.start()
        else:
            pl.when(pred)(copy.start)
        pending.append((copy, pred))

    def arrive(dst, arrival, pred=None):
        copy = pltpu.make_async_remote_copy(
            src_ref=dst, dst_ref=dst, send_sem=ssem.at[0], recv_sem=arrival,
            device_id=north, device_id_type=MESH,
        )
        if pred is None:
            copy.wait_recv()
        else:
            pl.when(pred)(copy.wait_recv)

    class Line:
        def __init__(self, slot):
            self.slot = slot
            self.plus = [None] + [new_recv() for _ in range(3)]
            self.minus = [None] + [new_recv() for _ in range(3)]

        def hop(self, d):
            if d >= 2:
                arrive(self.slot(jnp.maximum(z - d + 1, 0)), self.plus[d - 1], p >= d - 1)
            if d <= 3:
                src = self.slot(jnp.maximum(z - d + 1, 0))
                send(src, src, up, self.plus[d], (p >= d - 1) & (p <= 2))
            if d >= 2:
                arrive(self.slot(jnp.minimum(z + d - 1, 7)), self.minus[d - 1], p <= 4 - d)
            if d <= 3:
                src = self.slot(jnp.minimum(z + d - 1, 7))
                send(src, src, down, self.minus[d], (p <= 4 - d) & (p >= 1))

    class Ring:
        def __init__(self, slot, first, second):
            self.slot, self.first, self.second = slot, first, second
            self.sems = [new_recv() for _ in range(4)]

        def start(self):
            for dev, sem in ((north, self.sems[0]), (south, self.sems[1])):
                send(self.slot(y), self.slot(y), dev, sem)

        def forward(self):
            arrive(self.slot(yp), self.sems[0])
            send(self.first(yp), self.first(yp), north, self.sems[2])
            arrive(self.slot(yn), self.sems[1])
            send(self.second(yn), self.second(yn), south, self.sems[3])

        def finish(self):
            arrive(self.first(yo), self.sems[2])
            arrive(self.second(yo), self.sems[3])

    ld_g.wait()
    ld_t.wait()
    swap = table[0, r] != 0
    lo, hi = raw[:, 0:1024], raw[:, 1024:2048]
    for q in range(2):
        block = jnp.where(swap, hi, lo) if q == 0 else jnp.where(swap, lo, hi)
        for s in range(4):
            strips[4 * q + s] = block[:, 256 * s:256 * s + 256]
    gbuf[p, z, y] = strips[z]

    pl.semaphore_wait(barrier, len(near))

    asem = [new_recv() for _ in range(8)]
    for d in (4, 3, 5, 2, 6, 1, 7):
        zz = (z + d) % 8
        send(strips.at[zz], gbuf.at[zz % 4, z, y], fdev(zz, y), asem[d])

    def ring_of(s, lanes=slice(0, 256)):
        return Ring(
            lambda yy: gbuf.at[s, :, yy, :, lanes],
            lambda yy: gbuf.at[s, pl.ds(0, 4), yy, :, lanes],
            lambda yy: gbuf.at[s, pl.ds(4, 4), yy, :, lanes],
        )

    halves = [slice(0, 128), slice(128, 256)]
    rings_p = [ring_of(p, half) for half in halves]
    beside = p + 1 - 2 * (p % 2)
    others = [(p + 2) % 4, 3 - p]
    rings = [ring_of(s) for s in others]
    line_r = Line(lambda zz: abuf.at[zz % 4])
    line_g = Line(lambda zz: gbuf.at[zz % 4, :, y])
    ring_r = Ring(
        lambda yy: bbuf.at[yy],
        lambda yy: bbuf.at[yy, pl.ds(0, 32)],
        lambda yy: bbuf.at[yy, pl.ds(32, 32)],
    )

    ld_b.wait()
    ring_r.start()
    ld_a.wait()
    line_r.hop(1)
    for d in (1, 7, 2, 6, 3, 5, 4):
        arrive(gbuf.at[p, (z + 8 - d) % 8, y], asem[d])
    for ring in rings_p:
        ring.start()
    line_g.hop(1)
    line_r.hop(2)
    line_r.hop(3)
    line_g.hop(2)
    rings_p[0].forward()
    rings_p[1].forward()
    ring_r.forward()
    line_r.hop(4)
    line_g.hop(3)

    psem = [[new_recv() for _ in range(4)] for _ in range(2)]
    for h, lanes in enumerate(halves):
        rings_p[h].finish()
        lbuf[p, h] = jnp.dot(
            abuf[...].reshape(256, 1024), gbuf[p, :, :, :, lanes].reshape(1024, 128), preferred_element_type=F32
        ).astype(BF16)
        for d in (1, 3, 2):
            send(lbuf.at[p, h], lbuf.at[p, h], fdev(4 * g + (p + d) % 4, y), psem[h][d])
    rings[0].start()
    line_g.hop(4)
    rings[1].start()

    def add_squares(t, total):
        part = gbuf[p, t].reshape(128, 256).astype(F32)
        return total + jnp.sum(part * part, axis=0, keepdims=True)

    grad_squares = lax.fori_loop(0, 8, add_squares, jnp.zeros((1, 256), F32))
    grad_squares = 0.25 * jnp.sum(grad_squares, axis=1, keepdims=True)

    scale = (1.0 - BETA) / 1024
    my_z, my_y = 2 * p + y // 2, 2 * (y % 2)
    lanes = pl.ds(pl.multiple_of(128 * (y // 2), 128), 128)

    def statistics(s):
        mine = gbuf[s, my_z, pl.ds(my_y, 2)].reshape(64, 256)
        for t in range(4):
            rows = gbuf[s, pl.ds(2 * t, 2)].reshape(256, 256)
            lf[:, 256 * t:256 * t + 256] += scale * lax.dot_general(mine, rows, NT, preferred_element_type=F32)
        turned = gbuf[p, :, :, :, lanes].reshape(1024, 128).T
        wide[...] = jnp.dot(turned, gbuf[s].reshape(1024, 256), preferred_element_type=F32)
        cols = pl.ds(pl.multiple_of(256 * s, 256), 256)
        rf[:, cols] = BETA * rf[:, cols] + scale * wide[pl.ds(pl.multiple_of(64 * (y % 2), 64), 64), :]

    ld_l.wait()
    ld_r.wait()
    lf[...] = BETA * lf[...]
    statistics(p)
    ring_r.finish()

    def tile_part(s, h):
        cols = pl.ds(pl.multiple_of(256 * s + 128 * h, 128), 128)
        return lax.dot_general(lbuf[s, h], bbuf[:, :, cols].reshape(256, 128), NT, preferred_element_type=F32)

    prod = tile_part(p, 0) + tile_part(p, 1)
    for h in range(2):
        for d in (1, 3, 2):
            s = (p + 4 - d) % 4
            arrive(lbuf.at[s, h], psem[h][d])
            prod = prod + tile_part(s, h)
    pbuf[...] = prod.astype(BF16).reshape(4, 2, 32, 256)

    mycols = pl.ds(pl.multiple_of(256 * p, 256), 256)
    for q in range(4):
        for j in range(2):
            k, hz, hy = 2 * q + j, 2 * q + y // 2, 2 * (y % 2) + j
            itself = (hz == z) & (hy == y)
            src, place, arrival = pbuf.at[q, j], land.at[r, g, :, mycols], hsem.at[4 * g + p]
            away = pltpu.make_async_remote_copy(
                src_ref=src, dst_ref=place, send_sem=hsend.at[k], recv_sem=arrival,
                device_id=fdev(hz, hy), device_id_type=MESH,
            )
            here = pltpu.make_async_copy(src, place, arrival)
            pl.when(itself)(here.start)
            pl.when(jnp.logical_not(itself))(away.start)
            pending.append((away, jnp.logical_not(itself)))

    squares = jnp.sum(jnp.sum(prod * prod, axis=0, keepdims=True), axis=1, keepdims=True)
    row = lax.broadcasted_iota(jnp.int32, (8, 128), 0)
    sum_y[y] = jnp.where(row < 4, squares, grad_squares)
    ysem = [new_recv() for _ in range(4)]
    for d in (2, 1, 3):
        send(sum_y.at[y], sum_y.at[y], fdev(z, (y + d) % 4), ysem[d])
    rings[0].forward()
    bsem = [new_recv() for _ in range(4)]
    for d in range(1, 4):
        strip = gbuf.at[p, :, (y + d) % 4]
        send(strip, strip, fdev(4 * g + beside, y), bsem[d])
    for d in (1, 3, 2):
        arrive(sum_y.at[(y + 4 - d) % 4], ysem[d])
    sum_z[z] = sum_y[0] + sum_y[1] + sum_y[2] + sum_y[3]
    zsem = [new_recv() for _ in range(8)]
    for d in (4, 3, 5, 2, 6, 1, 7):
        send(sum_z.at[z], sum_z.at[z], fdev((z + d) % 8, y), zsem[d])

    order = (g, 1 - g)

    def rep_of(q, dx):
        return ((x + dx + 4) % 4) * 4 + (yl + q - 2 * yl * q) * 2 + c

    sib_waits = []

    def share(rr, k):
        sem = new_recv()
        ref = land.at[rr, order[k]]
        send(ref, ref, sib, sem)
        sib_waits.append((rr + 1 - 2 * c, k, sem))

    y_sem = [new_recv() for _ in range(2)]
    xsem = [[[new_recv() for _ in range(2)] for _ in range(4)] for _ in range(2)]
    for k in range(2):
        for q in range(4):
            arrive(land.at[r, order[k], :, pl.ds(256 * q, 256)], hsem.at[4 * order[k] + q])
        mine = land.at[r, order[k]]
        send(mine, mine, ylo, y_sem[k])
        for d in (1, 3, 2):
            send(mine, mine, {"rep": rep_of(0, d)}, xsem[0][d][k])
        share(r, k)
    for k in range(2):
        mine = land.at[r_ylo, order[k]]
        arrive(mine, y_sem[k])
        for d in (1, 3, 2):
            send(mine, mine, {"rep": rep_of(0, d)}, xsem[1][d][k])
        share(r_ylo, k)

    for d in (1, 7, 2, 6, 3, 5, 4):
        arrive(sum_z.at[(z + 8 - d) % 8], zsem[d])
    for q in range(2):
        total = sum_z[4 * q] + sum_z[4 * q + 1] + sum_z[4 * q + 2] + sum_z[4 * q + 3]
        norm = jnp.sqrt(total[4:5, 0:1]) / jnp.sqrt(total[0:1, 0:1] + EPSILON)
        ratio[r, q] = jnp.broadcast_to(norm, (8, 128))

    def tell(d, _):
        pltpu.make_async_remote_copy(
            src_ref=ratio.at[r], dst_ref=ratio.at[r], send_sem=tsem.at[0], recv_sem=tsem.at[1],
            device_id={"rep": (r + d) % 16}, device_id_type=MESH,
        ).start()
        return 0

    lax.fori_loop(1, 16, tell, 0)
    rings[1].forward()
    for d in (1, 2, 3):
        arrive(gbuf.at[beside, :, (y + d) % 4], bsem[d])
    statistics(beside)
    for d in (1, 3, 2):
        for k in range(2):
            arrive(land.at[rep_of(0, -d), order[k]], xsem[0][d][k])
            share(rep_of(0, -d), k)
    rings[0].finish()
    statistics(others[0])
    told = pltpu.make_async_remote_copy(
        src_ref=ratio.at[pl.ds(0, 15)], dst_ref=ratio.at[pl.ds(0, 15)], send_sem=tsem.at[0], recv_sem=tsem.at[1],
        device_id=north, device_id_type=MESH,
    )
    told.wait_recv()

    def emit(rr):
        swapped = table[0, rr] != 0
        scaled = [(land[rr, q].astype(F32) * ratio[rr, q, 0:1, 0:1]).astype(BF16) for q in range(2)]
        for k in range(2):
            cols = pl.ds(pl.multiple_of(rr * 2048 + 1024 * k, 1024), 1024)
            upd[:, cols] = jnp.where(swapped, scaled[1 - k], scaled[k])

    emit(r)
    emit(r_ylo)
    for d in (1, 3, 2):
        emit(rep_of(0, -d))
    for d in (1, 3, 2):
        for k in range(2):
            arrive(land.at[rep_of(1, -d), order[k]], xsem[1][d][k])
            share(rep_of(1, -d), k)
    rings[1].finish()
    statistics(others[1])
    for d in (1, 3, 2):
        emit(rep_of(1, -d))
    for rr, k, sem in sib_waits:
        arrive(land.at[rr, order[k]], sem)
        if k == 1:
            emit(rr)
    for copy, pred in pending:
        if pred is None:
            copy.wait_send()
        else:
            pl.when(pred)(copy.wait_send)
    told.wait_send()


def pinned(array):
    return pltpu.with_memory_space_constraint(array, pltpu.HBM)


def body(gradient, owner_table, left_factor, right_factor, left_root, right_root):
    vmem = pltpu.VMEM
    hbm = pl.BlockSpec(memory_space=pltpu.HBM)
    return pl.pallas_call(
        kernel,
        out_shape=(
            vmem((32, 32768), BF16),
            vmem((1, 64, 1024), F32),
            vmem((1, 64, 1024), F32),
        ),
        in_specs=[hbm] * 6,
        out_specs=(pl.BlockSpec(memory_space=pltpu.VMEM),) * 3,
        scratch_shapes=[
            pltpu.SMEM((2, 16), jnp.int32),
            vmem((32, 2048), BF16),
            vmem((8, 32, 256), BF16),
            vmem((4, 8, 4, 32, 256), BF16),
            vmem((4, 64, 1024), BF16),
            vmem((4, 64, 1024), BF16),
            vmem((4, 2, 256, 128), BF16),
            vmem((4, 2, 32, 256), BF16),
            vmem((16, 2, 32, 1024), BF16),
            vmem((128, 256), F32),
            vmem((4, 8, 128), F32),
            vmem((8, 8, 128), F32),
            vmem((16, 2, 8, 128), F32),
            pltpu.SemaphoreType.DMA((6,)),
            pltpu.SemaphoreType.DMA((112,)),
            pltpu.SemaphoreType.DMA((112,)),
            pltpu.SemaphoreType.DMA((8,)),
            pltpu.SemaphoreType.DMA((2,)),
            pltpu.SemaphoreType.DMA((8,)),
        ],
        compiler_params=pltpu.CompilerParams(
            collective_id=0, has_side_effects=True, vmem_limit_bytes=40 * 1024 * 1024
        ),
    )(
        pinned(gradient), pinned(owner_table.T), pinned(left_factor), pinned(right_factor),
        pinned(left_root), pinned(right_root),
    )


def solution(mesh):
    placed = (
        P("fsdp", "rep"),
        P(),
        P("rep", "fsdp", None),
        P("rep", "fsdp", None),
        P("rep", "fsdp", None),
        P("rep", "fsdp", None),
    )
    return jax.shard_map(
        body,
        mesh=mesh,
        in_specs=placed,
        out_specs=(P("fsdp", None), P("rep", "fsdp", None), P("rep", "fsdp", None)),
        check_vma=False,
    )
```

```python
import jax
import jax.numpy as jnp
from jax import lax
from jax.experimental import pallas as pl
from jax.experimental.pallas import tpu as pltpu
from jax.sharding import PartitionSpec as P

BETA = 0.9
EPSILON = 1e-06
MESH = pl.DeviceIdType.MESH
F32 = jnp.float32
BF16 = jnp.bfloat16
NT = (((1,), (1,)), ((), ()))


def kernel(
    grad_in, table_in, lf_in, rf_in, lr_in, rr_in,
    upd, lf_out, rf_out,
    table, raw, strips, gbuf, abuf, bbuf, lbuf, pbuf, land, wide, sum_y, sum_z, ratio,
    lsem, ssem, rsem, hsem, tsem, hsend,
):
    r = lax.axis_index("rep")
    f = lax.axis_index("fsdp")
    z, y = f // 4, f % 4
    g, p = z // 4, z % 4
    x, yl, c = r // 4, (r // 2) % 2, r % 2
    yn, yp, yo = (y + 1) % 4, (y + 3) % 4, (y + 2) % 4

    def fdev(zz, yy):
        return {"fsdp": zz * 4 + yy}

    up, down, north, south = fdev((z + 1) % 8, y), fdev((z + 7) % 8, y), fdev(z, yn), fdev(z, yp)
    up2, down2 = fdev((z + 2) % 8, y), fdev((z + 6) % 8, y)
    r_sib, r_ylo = r + 1 - 2 * c, r + 2 - 4 * yl
    sib, ylo = {"rep": r_sib}, {"rep": r_ylo}

    barrier = pltpu.get_barrier_semaphore()
    near = [fdev((z + d) % 8, y) for d in (1, 7, 2, 6, 3, 5, 4)] + [north, south]
    near += [{"rep": (r + d) % 16} for d in range(1, 16)]
    for dev in near:
        pl.semaphore_signal(barrier, inc=1, device_id=dev, device_id_type=MESH)

    def load(src, dst, k):
        copy = pltpu.make_async_copy(src, dst, lsem.at[k])
        copy.start()
        return copy

    ld_g = load(grad_in, raw, 0)
    ld_t = load(table_in, table, 5)
    ld_a = load(lr_in.at[0], abuf.at[p], 1)
    ld_b = load(rr_in.at[0], bbuf.at[y], 2)
    lf, rf = lf_out.at[0], rf_out.at[0]
    ld_l = load(lf_in.at[0], lf, 3)
    ld_r = load(rf_in.at[0], rf, 4)

    pending = []
    counter = [0, 0]

    def new_recv():
        counter[1] += 1
        return rsem.at[counter[1] - 1]

    def send(src, dst, dev, arrival, pred=None):
        copy = pltpu.make_async_remote_copy(
            src_ref=src, dst_ref=dst, send_sem=ssem.at[counter[0]], recv_sem=arrival,
            device_id=dev, device_id_type=MESH,
        )
        counter[0] += 1
        if pred is None:
            copy.start()
        else:
            pl.when(pred)(copy.start)
        pending.append((copy, pred))

    def arrive(dst, arrival, pred=None):
        copy = pltpu.make_async_remote_copy(
            src_ref=dst, dst_ref=dst, send_sem=ssem.at[0], recv_sem=arrival,
            device_id=north, device_id_type=MESH,
        )
        if pred is None:
            copy.wait_recv()
        else:
            pl.when(pred)(copy.wait_recv)

    class Line:
        def __init__(self, slot):
            self.slot = slot
            self.plus = [new_recv() for _ in range(4)]
            self.minus = [new_recv() for _ in range(4)]

        def below(self, d):
            return self.slot(jnp.maximum(z - d, 0))

        def above(self, d):
            return self.slot(jnp.minimum(z + d, 7))

        def start(self):
            mine = self.slot(z)
            send(mine, mine, up2, self.plus[2], p <= 1)
            send(mine, mine, down2, self.minus[2], p >= 2)
            send(mine, mine, up, self.plus[1], p <= 2)
            send(mine, mine, down, self.minus[1], p >= 1)

        def forward(self):
            arrive(self.below(2), self.plus[2], p >= 2)
            send(self.below(2), self.below(2), up, self.plus[3], p == 2)
            arrive(self.above(2), self.minus[2], p <= 1)
            send(self.above(2), self.above(2), down, self.minus[3], p == 1)

        def finish(self):
            arrive(self.below(1), self.plus[1], p >= 1)
            arrive(self.above(1), self.minus[1], p <= 2)
            arrive(self.below(3), self.plus[3], p == 3)
            arrive(self.above(3), self.minus[3], p == 0)

    class Ring:
        def __init__(self, slot, first, second):
            self.slot, self.first, self.second = slot, first, second
            self.sems = [new_recv() for _ in range(4)]

        def start(self):
            for dev, sem in ((north, self.sems[0]), (south, self.sems[1])):
                send(self.slot(y), self.slot(y), dev, sem)

        def forward(self):
            arrive(self.slot(yp), self.sems[0])
            send(self.first(yp), self.first(yp), north, self.sems[2])
            arrive(self.slot(yn), self.sems[1])
            send(self.second(yn), self.second(yn), south, self.sems[3])

        def finish(self):
            arrive(self.first(yo), self.sems[2])
            arrive(self.second(yo), self.sems[3])

    ld_g.wait()
    ld_t.wait()
    swap = table[0, r] != 0
    lo, hi = raw[:, 0:1024], raw[:, 1024:2048]
    for q in range(2):
        block = jnp.where(swap, hi, lo) if q == 0 else jnp.where(swap, lo, hi)
        for s in range(4):
            strips[4 * q + s] = block[:, 256 * s:256 * s + 256]
    gbuf[p, z, y] = strips[z]

    pl.semaphore_wait(barrier, len(near))

    asem = [new_recv() for _ in range(8)]
    for d in (4, 3, 5, 2, 6, 1, 7):
        zz = (z + d) % 8
        send(strips.at[zz], gbuf.at[zz % 4, z, y], fdev(zz, y), asem[d])

    def ring_of(s, lanes=slice(0, 256)):
        return Ring(
            lambda yy: gbuf.at[s, :, yy, :, lanes],
            lambda yy: gbuf.at[s, pl.ds(0, 4), yy, :, lanes],
            lambda yy: gbuf.at[s, pl.ds(4, 4), yy, :, lanes],
        )

    halves = [slice(0, 128), slice(128, 256)]
    rings_p = [ring_of(p, half) for half in halves]
    beside = p + 1 - 2 * (p % 2)
    others = [(p + 2) % 4, 3 - p]
    rings = [ring_of(s) for s in others]
    line_r = Line(lambda zz: abuf.at[zz % 4])
    line_g = Line(lambda zz: gbuf.at[zz % 4, :, y])
    ring_r = Ring(
        lambda yy: bbuf.at[yy],
        lambda yy: bbuf.at[yy, pl.ds(0, 32)],
        lambda yy: bbuf.at[yy, pl.ds(32, 32)],
    )

    ld_b.wait()
    ring_r.start()
    ld_a.wait()
    line_r.start()
    for d in (1, 7, 2, 6, 3, 5, 4):
        arrive(gbuf.at[p, (z + 8 - d) % 8, y], asem[d])
    for ring in rings_p:
        ring.start()
    line_g.start()
    line_r.forward()
    rings_p[0].forward()
    rings_p[1].forward()
    ring_r.forward()
    line_g.forward()
    rings[0].start()
    line_r.finish()

    lines_l = [Line(lambda zz, h=h: lbuf.at[zz % 4, h]) for h in range(2)]
    for h, lanes in enumerate(halves):
        rings_p[h].finish()
        lbuf[p, h] = jnp.dot(
            abuf[...].reshape(256, 1024), gbuf[p, :, :, :, lanes].reshape(1024, 128), preferred_element_type=F32
        ).astype(BF16)
        lines_l[h].start()
    lines_l[0].forward()

    def add_squares(t, total):
        part = gbuf[p, t].reshape(128, 256).astype(F32)
        return total + jnp.sum(part * part, axis=0, keepdims=True)

    grad_squares = lax.fori_loop(0, 8, add_squares, jnp.zeros((1, 256), F32))
    lines_l[1].forward()
    line_g.finish()
    grad_squares = 0.25 * jnp.sum(grad_squares, axis=1, keepdims=True)

    scale = (1.0 - BETA) / 1024
    my_z, my_y = 2 * p + y // 2, 2 * (y % 2)
    lanes = pl.ds(pl.multiple_of(128 * (y // 2), 128), 128)

    def statistics(s):
        mine = gbuf[s, my_z, pl.ds(my_y, 2)].reshape(64, 256)
        for t in range(4):
            rows = gbuf[s, pl.ds(2 * t, 2)].reshape(256, 256)
            lf[:, 256 * t:256 * t + 256] += scale * lax.dot_general(mine, rows, NT, preferred_element_type=F32)
        turned = gbuf[p, :, :, :, lanes].reshape(1024, 128).T
        wide[...] = jnp.dot(turned, gbuf[s].reshape(1024, 256), preferred_element_type=F32)
        cols = pl.ds(pl.multiple_of(256 * s, 256), 256)
        rf[:, cols] = BETA * rf[:, cols] + scale * wide[pl.ds(pl.multiple_of(64 * (y % 2), 64), 64), :]

    ld_l.wait()
    ld_r.wait()
    lf[...] = BETA * lf[...]
    statistics(p)
    ring_r.finish()
    rings[0].forward()

    def tile_part(s, h):
        cols = pl.ds(pl.multiple_of(256 * s + 128 * h, 128), 128)
        return lax.dot_general(lbuf[s, h], bbuf[:, :, cols].reshape(256, 128), NT, preferred_element_type=F32)

    prod = tile_part(p, 0) + tile_part(p, 1)
    for h in range(2):
        lines_l[h].finish()
        for d in range(1, 4):
            prod = prod + tile_part((p + d) % 4, h)
    pbuf[...] = prod.astype(BF16).reshape(4, 2, 32, 256)

    mycols = pl.ds(pl.multiple_of(256 * p, 256), 256)
    for q in range(4):
        for j in range(2):
            k, hz, hy = 2 * q + j, 2 * q + y // 2, 2 * (y % 2) + j
            itself = (hz == z) & (hy == y)
            src, place, arrival = pbuf.at[q, j], land.at[r, g, :, mycols], hsem.at[4 * g + p]
            away = pltpu.make_async_remote_copy(
                src_ref=src, dst_ref=place, send_sem=hsend.at[k], recv_sem=arrival,
                device_id=fdev(hz, hy), device_id_type=MESH,
            )
            here = pltpu.make_async_copy(src, place, arrival)
            pl.when(itself)(here.start)
            pl.when(jnp.logical_not(itself))(away.start)
            pending.append((away, jnp.logical_not(itself)))

    squares = jnp.sum(jnp.sum(prod * prod, axis=0, keepdims=True), axis=1, keepdims=True)
    row = lax.broadcasted_iota(jnp.int32, (8, 128), 0)
    sum_y[y] = jnp.where(row < 4, squares, grad_squares)
    ysem = [new_recv() for _ in range(4)]
    for d in (2, 1, 3):
        send(sum_y.at[y], sum_y.at[y], fdev(z, (y + d) % 4), ysem[d])
    for d in (1, 3, 2):
        arrive(sum_y.at[(y + 4 - d) % 4], ysem[d])
    sum_z[z] = sum_y[0] + sum_y[1] + sum_y[2] + sum_y[3]
    zsem = [new_recv() for _ in range(8)]
    for d in (4, 3, 5, 2, 6, 1, 7):
        send(sum_z.at[z], sum_z.at[z], fdev((z + d) % 8, y), zsem[d])

    order = (g, 1 - g)

    def rep_of(q, dx):
        return ((x + dx + 4) % 4) * 4 + (yl + q - 2 * yl * q) * 2 + c

    sib_waits = []

    def share(rr, k):
        sem = new_recv()
        ref = land.at[rr, order[k]]
        send(ref, ref, sib, sem)
        sib_waits.append((rr + 1 - 2 * c, k, sem))

    y_sem = [new_recv() for _ in range(2)]
    xsem = [[[new_recv() for _ in range(2)] for _ in range(4)] for _ in range(2)]
    for k in range(2):
        for q in range(4):
            arrive(land.at[r, order[k], :, pl.ds(256 * q, 256)], hsem.at[4 * order[k] + q])
        mine = land.at[r, order[k]]
        send(mine, mine, ylo, y_sem[k])
        for d in (2, 1, 3):
            send(mine, mine, {"rep": rep_of(0, d)}, xsem[0][d][k])
        share(r, k)
    rings[1].start()
    bsem = [new_recv() for _ in range(4)]
    for d in range(1, 4):
        strip = gbuf.at[p, :, (y + d) % 4]
        send(strip, strip, fdev(4 * g + beside, y), bsem[d])
    for k in range(2):
        mine = land.at[r_ylo, order[k]]
        arrive(mine, y_sem[k])
        for d in (2, 1, 3):
            send(mine, mine, {"rep": rep_of(0, d)}, xsem[1][d][k])
        share(r_ylo, k)
    for k in range(2):
        across = land.at[rep_of(0, 2), order[k]]
        arrive(across, xsem[0][2][k])
        share(rep_of(0, 2), k)

    for d in (1, 7, 2, 6, 3, 5, 4):
        arrive(sum_z.at[(z + 8 - d) % 8], zsem[d])
    for q in range(2):
        total = sum_z[4 * q] + sum_z[4 * q + 1] + sum_z[4 * q + 2] + sum_z[4 * q + 3]
        norm = jnp.sqrt(total[4:5, 0:1]) / jnp.sqrt(total[0:1, 0:1] + EPSILON)
        ratio[r, q] = jnp.broadcast_to(norm, (8, 128))

    def tell(d, _):
        pltpu.make_async_remote_copy(
            src_ref=ratio.at[r], dst_ref=ratio.at[r], send_sem=tsem.at[0], recv_sem=tsem.at[1],
            device_id={"rep": (r + d) % 16}, device_id_type=MESH,
        ).start()
        return 0

    lax.fori_loop(1, 16, tell, 0)
    rings[1].forward()
    for d in (1, 3):
        for k in range(2):
            arrive(land.at[rep_of(0, -d), order[k]], xsem[0][d][k])
            share(rep_of(0, -d), k)
    rings[0].finish()
    statistics(others[0])
    told = pltpu.make_async_remote_copy(
        src_ref=ratio.at[pl.ds(0, 15)], dst_ref=ratio.at[pl.ds(0, 15)], send_sem=tsem.at[0], recv_sem=tsem.at[1],
        device_id=north, device_id_type=MESH,
    )
    told.wait_recv()

    def emit(rr):
        swapped = table[0, rr] != 0
        scaled = [(land[rr, q].astype(F32) * ratio[rr, q, 0:1, 0:1]).astype(BF16) for q in range(2)]
        for k in range(2):
            cols = pl.ds(pl.multiple_of(rr * 2048 + 1024 * k, 1024), 1024)
            upd[:, cols] = jnp.where(swapped, scaled[1 - k], scaled[k])

    emit(r)
    emit(r_ylo)
    for d in (1, 3, 2):
        emit(rep_of(0, -d))
    for d in (1, 3, 2):
        for k in range(2):
            arrive(land.at[rep_of(1, -d), order[k]], xsem[1][d][k])
            share(rep_of(1, -d), k)
    for d in (1, 2, 3):
        arrive(gbuf.at[beside, :, (y + d) % 4], bsem[d])
    statistics(beside)
    rings[1].finish()
    statistics(others[1])
    for d in (1, 3, 2):
        emit(rep_of(1, -d))
    for rr, k, sem in sib_waits:
        arrive(land.at[rr, order[k]], sem)
        if k == 1:
            emit(rr)
    for copy, pred in pending:
        if pred is None:
            copy.wait_send()
        else:
            pl.when(pred)(copy.wait_send)
    told.wait_send()


def deliver(upd, left, right, upd_out, left_out, right_out, sem):
    pairs = [(upd.at[pl.ds(16 * k, 16)], upd_out.at[pl.ds(16 * k, 16)]) for k in range(2)]
    pairs += [(left, left_out), (right, right_out)]
    copies = [pltpu.make_async_copy(src, dst, sem.at[k]) for k, (src, dst) in enumerate(pairs)]
    for copy in copies:
        copy.start()
    for copy in copies:
        copy.wait()


def pinned(array):
    return pltpu.with_memory_space_constraint(array, pltpu.HBM)


def body(gradient, owner_table, left_factor, right_factor, left_root, right_root):
    vmem = pltpu.VMEM
    hbm = pl.BlockSpec(memory_space=pltpu.HBM)
    results = pl.pallas_call(
        kernel,
        out_shape=(
            vmem((32, 32768), BF16),
            vmem((1, 64, 1024), F32),
            vmem((1, 64, 1024), F32),
        ),
        in_specs=[hbm] * 6,
        out_specs=(pl.BlockSpec(memory_space=pltpu.VMEM),) * 3,
        scratch_shapes=[
            pltpu.SMEM((2, 16), jnp.int32),
            vmem((32, 2048), BF16),
            vmem((8, 32, 256), BF16),
            vmem((4, 8, 4, 32, 256), BF16),
            vmem((4, 64, 1024), BF16),
            vmem((4, 64, 1024), BF16),
            vmem((4, 2, 256, 128), BF16),
            vmem((4, 2, 32, 256), BF16),
            vmem((16, 2, 32, 1024), BF16),
            vmem((128, 256), F32),
            vmem((4, 8, 128), F32),
            vmem((8, 8, 128), F32),
            vmem((16, 2, 8, 128), F32),
            pltpu.SemaphoreType.DMA((6,)),
            pltpu.SemaphoreType.DMA((112,)),
            pltpu.SemaphoreType.DMA((112,)),
            pltpu.SemaphoreType.DMA((8,)),
            pltpu.SemaphoreType.DMA((2,)),
            pltpu.SemaphoreType.DMA((8,)),
        ],
        compiler_params=pltpu.CompilerParams(
            collective_id=0, has_side_effects=True, vmem_limit_bytes=40 * 1024 * 1024
        ),
    )(
        pinned(gradient), pinned(owner_table.T), pinned(left_factor), pinned(right_factor),
        pinned(left_root), pinned(right_root),
    )
    return pl.pallas_call(
        deliver,
        out_shape=tuple(pltpu.HBM(a.shape, a.dtype) for a in results),
        in_specs=[pl.BlockSpec(memory_space=pltpu.VMEM)] * 3,
        out_specs=(hbm,) * 3,
        scratch_shapes=[pltpu.SemaphoreType.DMA((6,))],
        compiler_params=pltpu.CompilerParams(vmem_limit_bytes=40 * 1024 * 1024),
    )(*[pltpu.with_memory_space_constraint(a, pltpu.VMEM) for a in results])


def solution(mesh):
    placed = (
        P("fsdp", "rep"),
        P(),
        P("rep", "fsdp", None),
        P("rep", "fsdp", None),
        P("rep", "fsdp", None),
        P("rep", "fsdp", None),
    )
    return jax.shard_map(
        body,
        mesh=mesh,
        in_specs=placed,
        out_specs=(P("fsdp", None), P("rep", "fsdp", None), P("rep", "fsdp", None)),
        check_vma=False,
    )
```

```python
import jax
import jax.numpy as jnp
from jax import lax
from jax.experimental import pallas as pl
from jax.experimental.pallas import tpu as pltpu
from jax.sharding import PartitionSpec as P

BETA = 0.9
EPSILON = 1e-06
MESH = pl.DeviceIdType.MESH
F32 = jnp.float32
BF16 = jnp.bfloat16
NT = (((1,), (1,)), ((), ()))


def kernel(
    grad_in, table_in, lf_in, rf_in, lr_in, rr_in,
    upd, lf_out, rf_out,
    table, raw, strips, gbuf, abuf, bbuf, lbuf, pbuf, land, wide, sum_y, sum_z, ratio,
    lsem, ssem, rsem, hsem, tsem, hsend,
):
    r = lax.axis_index("rep")
    f = lax.axis_index("fsdp")
    z, y = f // 4, f % 4
    g, p = z // 4, z % 4
    x, yl, c = r // 4, (r // 2) % 2, r % 2
    yn, yp, yo = (y + 1) % 4, (y + 3) % 4, (y + 2) % 4

    def fdev(zz, yy):
        return {"fsdp": zz * 4 + yy}

    up, down, north, south = fdev((z + 1) % 8, y), fdev((z + 7) % 8, y), fdev(z, yn), fdev(z, yp)
    up2, down2 = fdev((z + 2) % 8, y), fdev((z + 6) % 8, y)
    r_sib, r_ylo = r + 1 - 2 * c, r + 2 - 4 * yl
    sib, ylo = {"rep": r_sib}, {"rep": r_ylo}

    barrier = pltpu.get_barrier_semaphore()
    near = [fdev((z + d) % 8, y) for d in (1, 7, 2, 6, 3, 5, 4)] + [north, south]
    near += [{"rep": (r + d) % 16} for d in range(1, 16)]
    for dev in near:
        pl.semaphore_signal(barrier, inc=1, device_id=dev, device_id_type=MESH)

    def load(src, dst, k):
        copy = pltpu.make_async_copy(src, dst, lsem.at[k])
        copy.start()
        return copy

    ld_g = load(grad_in, raw, 0)
    ld_t = load(table_in, table, 5)
    ld_a = load(lr_in.at[0], abuf.at[p], 1)
    ld_b = load(rr_in.at[0], bbuf.at[y], 2)
    lf, rf = lf_out.at[0], rf_out.at[0]
    ld_l = load(lf_in.at[0], lf, 3)
    ld_r = load(rf_in.at[0], rf, 4)

    pending = []
    counter = [0, 0]

    def new_recv():
        counter[1] += 1
        return rsem.at[counter[1] - 1]

    def send(src, dst, dev, arrival, pred=None):
        copy = pltpu.make_async_remote_copy(
            src_ref=src, dst_ref=dst, send_sem=ssem.at[counter[0]], recv_sem=arrival,
            device_id=dev, device_id_type=MESH,
        )
        counter[0] += 1
        if pred is None:
            copy.start()
        else:
            pl.when(pred)(copy.start)
        pending.append((copy, pred))

    def arrive(dst, arrival, pred=None):
        copy = pltpu.make_async_remote_copy(
            src_ref=dst, dst_ref=dst, send_sem=ssem.at[0], recv_sem=arrival,
            device_id=north, device_id_type=MESH,
        )
        if pred is None:
            copy.wait_recv()
        else:
            pl.when(pred)(copy.wait_recv)

    class Line:
        def __init__(self, slot):
            self.slot = slot
            self.plus = [new_recv() for _ in range(4)]
            self.minus = [new_recv() for _ in range(4)]

        def below(self, d):
            return self.slot(jnp.maximum(z - d, 0))

        def above(self, d):
            return self.slot(jnp.minimum(z + d, 7))

        def start(self):
            mine = self.slot(z)
            send(mine, mine, up2, self.plus[2], p <= 1)
            send(mine, mine, down2, self.minus[2], p >= 2)
            send(mine, mine, up, self.plus[1], p <= 2)
            send(mine, mine, down, self.minus[1], p >= 1)

        def forward(self):
            arrive(self.below(2), self.plus[2], p >= 2)
            send(self.below(2), self.below(2), up, self.plus[3], p == 2)
            arrive(self.above(2), self.minus[2], p <= 1)
            send(self.above(2), self.above(2), down, self.minus[3], p == 1)

        def finish(self):
            arrive(self.below(1), self.plus[1], p >= 1)
            arrive(self.above(1), self.minus[1], p <= 2)
            arrive(self.below(3), self.plus[3], p == 3)
            arrive(self.above(3), self.minus[3], p == 0)

    class Ring:
        def __init__(self, slot, first, second):
            self.slot, self.first, self.second = slot, first, second
            self.sems = [new_recv() for _ in range(4)]

        def start(self):
            for dev, sem in ((north, self.sems[0]), (south, self.sems[1])):
                send(self.slot(y), self.slot(y), dev, sem)

        def forward(self):
            arrive(self.slot(yp), self.sems[0])
            send(self.first(yp), self.first(yp), north, self.sems[2])
            arrive(self.slot(yn), self.sems[1])
            send(self.second(yn), self.second(yn), south, self.sems[3])

        def finish(self):
            arrive(self.first(yo), self.sems[2])
            arrive(self.second(yo), self.sems[3])

    ld_g.wait()
    ld_t.wait()
    swap = table[0, r] != 0
    lo, hi = raw[:, 0:1024], raw[:, 1024:2048]
    for q in range(2):
        block = jnp.where(swap, hi, lo) if q == 0 else jnp.where(swap, lo, hi)
        for s in range(4):
            strips[4 * q + s] = block[:, 256 * s:256 * s + 256]
    gbuf[p, z, y] = strips[z]

    pl.semaphore_wait(barrier, len(near))

    asem = [new_recv() for _ in range(8)]
    for d in (4, 3, 5, 2, 6, 1, 7):
        zz = (z + d) % 8
        send(strips.at[zz], gbuf.at[zz % 4, z, y], fdev(zz, y), asem[d])

    def ring_of(s, lanes=slice(0, 256)):
        return Ring(
            lambda yy: gbuf.at[s, :, yy, :, lanes],
            lambda yy: gbuf.at[s, pl.ds(0, 4), yy, :, lanes],
            lambda yy: gbuf.at[s, pl.ds(4, 4), yy, :, lanes],
        )

    halves = [slice(0, 128), slice(128, 256)]
    rings_p = [ring_of(p, half) for half in halves]
    beside = p + 1 - 2 * (p % 2)
    others = [(p + 2) % 4, 3 - p]
    rings = [ring_of(s) for s in others]
    line_r = Line(lambda zz: abuf.at[zz % 4])
    cross = [new_recv() for _ in range(2)]
    far, last = gbuf.at[others[0], :, y], gbuf.at[others[1], :, y]
    ring_r = Ring(
        lambda yy: bbuf.at[yy],
        lambda yy: bbuf.at[yy, pl.ds(0, 32)],
        lambda yy: bbuf.at[yy, pl.ds(32, 32)],
    )

    ld_b.wait()
    ring_r.start()
    ld_a.wait()
    line_r.start()
    for d in (1, 7, 2, 6, 3, 5, 4):
        arrive(gbuf.at[p, (z + 8 - d) % 8, y], asem[d])
    for ring in rings_p:
        ring.start()
    send(gbuf.at[p, :, y], gbuf.at[p, :, y], fdev(4 * g + others[0], y), cross[0])
    line_r.forward()
    rings_p[0].forward()
    rings_p[1].forward()
    ring_r.forward()
    arrive(far, cross[0])
    rings[0].start()
    line_r.finish()

    lines_l = [Line(lambda zz, h=h: lbuf.at[zz % 4, h]) for h in range(2)]
    for h, lanes in enumerate(halves):
        rings_p[h].finish()
        lbuf[p, h] = jnp.dot(
            abuf[...].reshape(256, 1024), gbuf[p, :, :, :, lanes].reshape(1024, 128), preferred_element_type=F32
        ).astype(BF16)
        lines_l[h].start()
    lines_l[0].forward()

    def add_squares(t, total):
        part = gbuf[p, t].reshape(128, 256).astype(F32)
        return total + jnp.sum(part * part, axis=0, keepdims=True)

    grad_squares = lax.fori_loop(0, 8, add_squares, jnp.zeros((1, 256), F32))
    lines_l[1].forward()
    send(far, far, fdev(4 * g + beside, y), cross[1])
    grad_squares = 0.25 * jnp.sum(grad_squares, axis=1, keepdims=True)

    scale = (1.0 - BETA) / 1024
    my_z, my_y = 2 * p + y // 2, 2 * (y % 2)
    lanes = pl.ds(pl.multiple_of(128 * (y // 2), 128), 128)

    def statistics(s):
        mine = gbuf[s, my_z, pl.ds(my_y, 2)].reshape(64, 256)
        for t in range(4):
            rows = gbuf[s, pl.ds(2 * t, 2)].reshape(256, 256)
            lf[:, 256 * t:256 * t + 256] += scale * lax.dot_general(mine, rows, NT, preferred_element_type=F32)
        turned = gbuf[p, :, :, :, lanes].reshape(1024, 128).T
        wide[...] = jnp.dot(turned, gbuf[s].reshape(1024, 256), preferred_element_type=F32)
        cols = pl.ds(pl.multiple_of(256 * s, 256), 256)
        rf[:, cols] = BETA * rf[:, cols] + scale * wide[pl.ds(pl.multiple_of(64 * (y % 2), 64), 64), :]

    ld_l.wait()
    ld_r.wait()
    lf[...] = BETA * lf[...]
    statistics(p)
    ring_r.finish()
    rings[0].forward()

    def tile_part(s, h):
        cols = pl.ds(pl.multiple_of(256 * s + 128 * h, 128), 128)
        return lax.dot_general(lbuf[s, h], bbuf[:, :, cols].reshape(256, 128), NT, preferred_element_type=F32)

    prod = tile_part(p, 0) + tile_part(p, 1)
    for h in range(2):
        lines_l[h].finish()
        for d in range(1, 4):
            prod = prod + tile_part((p + d) % 4, h)
    pbuf[...] = prod.astype(BF16).reshape(4, 2, 32, 256)

    mycols = pl.ds(pl.multiple_of(256 * p, 256), 256)
    for q in range(4):
        for j in range(2):
            k, hz, hy = 2 * q + j, 2 * q + y // 2, 2 * (y % 2) + j
            itself = (hz == z) & (hy == y)
            src, place, arrival = pbuf.at[q, j], land.at[r, g, :, mycols], hsem.at[4 * g + p]
            away = pltpu.make_async_remote_copy(
                src_ref=src, dst_ref=place, send_sem=hsend.at[k], recv_sem=arrival,
                device_id=fdev(hz, hy), device_id_type=MESH,
            )
            here = pltpu.make_async_copy(src, place, arrival)
            pl.when(itself)(here.start)
            pl.when(jnp.logical_not(itself))(away.start)
            pending.append((away, jnp.logical_not(itself)))

    squares = jnp.sum(jnp.sum(prod * prod, axis=0, keepdims=True), axis=1, keepdims=True)
    row = lax.broadcasted_iota(jnp.int32, (8, 128), 0)
    sum_y[y] = jnp.where(row < 4, squares, grad_squares)
    ysem = [new_recv() for _ in range(4)]
    for d in (2, 1, 3):
        send(sum_y.at[y], sum_y.at[y], fdev(z, (y + d) % 4), ysem[d])
    for d in (1, 3, 2):
        arrive(sum_y.at[(y + 4 - d) % 4], ysem[d])
    sum_z[z] = sum_y[0] + sum_y[1] + sum_y[2] + sum_y[3]
    zsem = [new_recv() for _ in range(8)]
    for d in (4, 3, 5, 2, 6, 1, 7):
        send(sum_z.at[z], sum_z.at[z], fdev((z + d) % 8, y), zsem[d])

    arrive(last, cross[1])
    rings[1].start()

    order = (g, 1 - g)

    def rep_of(q, dx):
        return ((x + dx + 4) % 4) * 4 + (yl + q - 2 * yl * q) * 2 + c

    sib_waits = []

    def share(rr, k):
        sem = new_recv()
        ref = land.at[rr, order[k]]
        send(ref, ref, sib, sem)
        sib_waits.append((rr + 1 - 2 * c, k, sem))

    y_sem = [new_recv() for _ in range(2)]
    xsem = [[[new_recv() for _ in range(2)] for _ in range(4)] for _ in range(2)]
    for k in range(2):
        for q in range(4):
            arrive(land.at[r, order[k], :, pl.ds(256 * q, 256)], hsem.at[4 * order[k] + q])
        mine = land.at[r, order[k]]
        send(mine, mine, ylo, y_sem[k])
        for d in (2, 1, 3):
            send(mine, mine, {"rep": rep_of(0, d)}, xsem[0][d][k])
        share(r, k)
    bsem = [new_recv() for _ in range(4)]
    for d in range(4):
        strip = gbuf.at[p, :, (y + d) % 4]
        send(strip, strip, fdev(4 * g + beside, y), bsem[d])
    for k in range(2):
        mine = land.at[r_ylo, order[k]]
        arrive(mine, y_sem[k])
        for d in (2, 1, 3):
            send(mine, mine, {"rep": rep_of(0, d)}, xsem[1][d][k])
        share(r_ylo, k)
    for k in range(2):
        across = land.at[rep_of(0, 2), order[k]]
        arrive(across, xsem[0][2][k])
        share(rep_of(0, 2), k)

    rings[1].forward()

    for d in (1, 7, 2, 6, 3, 5, 4):
        arrive(sum_z.at[(z + 8 - d) % 8], zsem[d])
    for q in range(2):
        total = sum_z[4 * q] + sum_z[4 * q + 1] + sum_z[4 * q + 2] + sum_z[4 * q + 3]
        norm = jnp.sqrt(total[4:5, 0:1]) / jnp.sqrt(total[0:1, 0:1] + EPSILON)
        ratio[r, q] = jnp.broadcast_to(norm, (8, 128))

    def tell(d, _):
        pltpu.make_async_remote_copy(
            src_ref=ratio.at[r], dst_ref=ratio.at[r], send_sem=tsem.at[0], recv_sem=tsem.at[1],
            device_id={"rep": (r + d) % 16}, device_id_type=MESH,
        ).start()
        return 0

    lax.fori_loop(1, 16, tell, 0)
    for d in (1, 3):
        for k in range(2):
            arrive(land.at[rep_of(0, -d), order[k]], xsem[0][d][k])
            share(rep_of(0, -d), k)
    rings[0].finish()
    statistics(others[0])
    told = pltpu.make_async_remote_copy(
        src_ref=ratio.at[pl.ds(0, 15)], dst_ref=ratio.at[pl.ds(0, 15)], send_sem=tsem.at[0], recv_sem=tsem.at[1],
        device_id=north, device_id_type=MESH,
    )
    told.wait_recv()

    def emit(rr):
        swapped = table[0, rr] != 0
        scaled = [(land[rr, q].astype(F32) * ratio[rr, q, 0:1, 0:1]).astype(BF16) for q in range(2)]
        for k in range(2):
            cols = pl.ds(pl.multiple_of(rr * 2048 + 1024 * k, 1024), 1024)
            upd[:, cols] = jnp.where(swapped, scaled[1 - k], scaled[k])

    emit(r)
    emit(r_ylo)
    for d in (1, 3, 2):
        emit(rep_of(0, -d))
    for d in (1, 3, 2):
        for k in range(2):
            arrive(land.at[rep_of(1, -d), order[k]], xsem[1][d][k])
            share(rep_of(1, -d), k)
    for d in range(4):
        arrive(gbuf.at[beside, :, (y + d) % 4], bsem[d])
    statistics(beside)
    rings[1].finish()
    statistics(others[1])
    for d in (1, 3, 2):
        emit(rep_of(1, -d))
    for rr, k, sem in sib_waits:
        arrive(land.at[rr, order[k]], sem)
        if k == 1:
            emit(rr)
    for copy, pred in pending:
        if pred is None:
            copy.wait_send()
        else:
            pl.when(pred)(copy.wait_send)
    told.wait_send()


def deliver(upd, left, right, upd_out, left_out, right_out, sem):
    pairs = [(upd.at[pl.ds(16 * k, 16)], upd_out.at[pl.ds(16 * k, 16)]) for k in range(2)]
    pairs += [(left, left_out), (right, right_out)]
    copies = [pltpu.make_async_copy(src, dst, sem.at[k]) for k, (src, dst) in enumerate(pairs)]
    for copy in copies:
        copy.start()
    for copy in copies:
        copy.wait()


def pinned(array):
    return pltpu.with_memory_space_constraint(array, pltpu.HBM)


def body(gradient, owner_table, left_factor, right_factor, left_root, right_root):
    vmem = pltpu.VMEM
    hbm = pl.BlockSpec(memory_space=pltpu.HBM)
    results = pl.pallas_call(
        kernel,
        out_shape=(
            vmem((32, 32768), BF16),
            vmem((1, 64, 1024), F32),
            vmem((1, 64, 1024), F32),
        ),
        in_specs=[hbm] * 6,
        out_specs=(pl.BlockSpec(memory_space=pltpu.VMEM),) * 3,
        scratch_shapes=[
            pltpu.SMEM((2, 16), jnp.int32),
            vmem((32, 2048), BF16),
            vmem((8, 32, 256), BF16),
            vmem((4, 8, 4, 32, 256), BF16),
            vmem((4, 64, 1024), BF16),
            vmem((4, 64, 1024), BF16),
            vmem((4, 2, 256, 128), BF16),
            vmem((4, 2, 32, 256), BF16),
            vmem((16, 2, 32, 1024), BF16),
            vmem((128, 256), F32),
            vmem((4, 8, 128), F32),
            vmem((8, 8, 128), F32),
            vmem((16, 2, 8, 128), F32),
            pltpu.SemaphoreType.DMA((6,)),
            pltpu.SemaphoreType.DMA((112,)),
            pltpu.SemaphoreType.DMA((112,)),
            pltpu.SemaphoreType.DMA((8,)),
            pltpu.SemaphoreType.DMA((2,)),
            pltpu.SemaphoreType.DMA((8,)),
        ],
        compiler_params=pltpu.CompilerParams(
            collective_id=0, has_side_effects=True, vmem_limit_bytes=40 * 1024 * 1024
        ),
    )(
        pinned(gradient), pinned(owner_table.T), pinned(left_factor), pinned(right_factor),
        pinned(left_root), pinned(right_root),
    )
    return pl.pallas_call(
        deliver,
        out_shape=tuple(pltpu.HBM(a.shape, a.dtype) for a in results),
        in_specs=[pl.BlockSpec(memory_space=pltpu.VMEM)] * 3,
        out_specs=(hbm,) * 3,
        scratch_shapes=[pltpu.SemaphoreType.DMA((6,))],
        compiler_params=pltpu.CompilerParams(vmem_limit_bytes=40 * 1024 * 1024),
    )(*[pltpu.with_memory_space_constraint(a, pltpu.VMEM) for a in results])


def solution(mesh):
    placed = (
        P("fsdp", "rep"),
        P(),
        P("rep", "fsdp", None),
        P("rep", "fsdp", None),
        P("rep", "fsdp", None),
        P("rep", "fsdp", None),
    )
    return jax.shard_map(
        body,
        mesh=mesh,
        in_specs=placed,
        out_specs=(P("fsdp", None), P("rep", "fsdp", None), P("rep", "fsdp", None)),
        check_vma=False,
    )
```
